1024 devices in a mesh: pair: 32 (over x, y_hi, core), virt: 32 (over y_lo, z).
Axes of the slice: x: 8, y: 8 (y_hi: 2, y_lo: 4; y = y_hi * 4 + y_lo), z: 8, core: 2. Of those that a mesh axis runs over, the one named last changes fastest.
Arguments:
- amplitudes: bfloat16 [36864, 2048], P(('pair', 'virt')), may hold values from -6 to 6
- integrals: bfloat16 [2048, 16384], P(None, 'virt'), may hold values from -0.125 to 0.125
- amp_pattern: int32 [32, 32, 2], replicated, may hold values 0 or 1
- int_pattern: int32 [2, 16], replicated, may hold values 0 or 1
Outputs:
- residual: bfloat16 [36864, 16384], P('pair', 'virt')
The draws below stay inside these ranges and needn't reach their ends.
All inputs are finite; a program needn't handle non-finite values.
Results may differ from the reference program's by a relative error of at most 0.005.
Values may be sent and summed in bfloat16 or wider, within the bound.
No kernel may reach another device: no remote copies, remote signals or barrier semaphores. Data moves between devices by JAX's collectives and lax.ppermute only.
A program may use at most 64 MiB of HBM per device.

```python
import jax
import jax.numpy as jnp
from jax import lax

TP = 1024
NB = 2
KCD = 2048
AB = 16384
NABT = 16
OCC_DEV = 6
NOCC = 192
NBLK = 32
NROWS = 36864


def touch_ends(result, key, least, top_value):
    shape = result.shape
    spot = [jax.random.randint(jax.random.fold_in(key, axis), (), 0, shape[axis]) for axis in range(len(shape))]
    result = result.at[tuple(spot)].set(least)
    longest = shape.index(max(shape))
    spot[longest] = (spot[longest] + 1) % shape[longest]
    return result.at[tuple(spot)].set(top_value)


def level_of(key, dims, split, least, high):
    factor_of = 1.0
    for dim, blocks in split:
        steps = jax.random.uniform(jax.random.fold_in(jax.random.fold_in(key, 6), dim), (blocks,), jnp.float32, least / len(split), high / len(split))
        factor_of = factor_of * jnp.repeat(jnp.exp(steps), dims[dim] // blocks).reshape((-1,) + (1,) * (len(dims) - 1 - dim))
    return factor_of


def noise(key, extent, deviation, bound, split=(), kind=jnp.bfloat16):
    drawn = deviation * jax.random.normal(key, extent, jnp.float32)
    if split:
        drawn = drawn * level_of(key, extent, split, -0.22, 0.18)
    return jnp.clip(drawn, -bound, bound).astype(kind)


def setup_inputs(seed: int = 0) -> dict:
    splits = jax.random.split(jax.random.key(seed), 5)
    return {
        "amplitudes": noise(splits[0], (NROWS, KCD), 1.0, 6.0, ((0, 1024),)),
        "integrals": noise(splits[1], (KCD, AB), KCD ** -0.5, 0.125, ((1, 32),)),
        "amp_pattern": touch_ends((jax.random.randint(splits[2], (NBLK, NBLK, NB), 0, 4) < 3).astype(jnp.int32), jax.random.fold_in(splits[2], 1), 0, 1),
        "int_pattern": touch_ends((jax.random.randint(splits[3], (NB, NABT), 0, 4) < 3).astype(jnp.int32), jax.random.fold_in(splits[3], 1), 0, 1),
    }


def reference(amplitudes, integrals, amp_pattern, int_pattern):
    row_ids = jnp.arange(NROWS)
    occ_first = row_ids // NOCC
    occ_second = row_ids % NOCC
    row_mask = amp_pattern[occ_first // OCC_DEV, occ_second // OCC_DEV, :]
    amp_mask = jnp.repeat(row_mask, TP, axis=1).astype(jnp.bfloat16)
    screened_amp = amplitudes * amp_mask
    col_ids = jnp.arange(AB)
    col_mask = int_pattern[:, col_ids // TP]
    int_mask = jnp.repeat(col_mask, TP, axis=0).astype(jnp.bfloat16)
    screened_int = integrals * int_mask
    ladder = jnp.dot(screened_amp.astype(jnp.float32), screened_int.astype(jnp.float32), precision=lax.Precision.HIGHEST)
    ladder = lax.optimization_barrier(ladder.astype(jnp.bfloat16)).astype(jnp.float32)
    mirror = jnp.transpose(ladder.reshape(NOCC, NOCC, AB), (1, 0, 2)).reshape(NROWS, AB)
    return (ladder - mirror).astype(jnp.bfloat16)
```

```python
import jax
import jax.numpy as jnp
from jax import lax
from jax.sharding import Mesh, PartitionSpec as P

TP = 1024
OCC = 6
NY = 4
NZ = 8
NP = 32
AXES = ("x", "yh", "core", "y", "z")
PAIR = ("x", "yh", "core")
VIRT = ("y", "z")


def body(amplitudes, integrals, amp_pattern, int_pattern):
    rows, kcd = amplitudes.shape
    cols = integrals.shape[1]
    tiles = kcd // TP
    p = lax.axis_index(PAIR)
    v = lax.axis_index(VIRT)
    z = lax.axis_index("z")
    second = (v * rows + jnp.arange(rows)) % (OCC * NP) // OCC
    block_mask = lax.dynamic_index_in_dim(amp_pattern, p, 0, keepdims=False)
    picks = (second[:, None] == jnp.arange(NP)[None, :]).astype(jnp.float32)
    row_mask = jnp.dot(picks, block_mask.astype(jnp.float32)).astype(jnp.bfloat16)
    screened = amplitudes * jnp.repeat(row_mask, TP, axis=1)
    col_mask = lax.dynamic_index_in_dim(int_pattern, v * cols // TP, 1, keepdims=False)
    weighted = integrals * jnp.repeat(col_mask, TP).astype(jnp.bfloat16)[:, None]

    packed = jnp.concatenate([screened[:, t * TP : (t + 1) * TP] for t in range(tiles)], 0)
    gathered = lax.all_gather(packed, "y", axis=0, tiled=False)
    chunk = (
        gathered.reshape(NY, tiles, rows, TP).transpose(0, 2, 1, 3).reshape(NY * rows, kcd)
    )

    up = [(i, (i + 1) % NZ) for i in range(NZ)]
    down = [(i, (i - 1) % NZ) for i in range(NZ)]

    def ladder_of(c):
        return jnp.dot(c, weighted, preferred_element_type=jnp.float32).astype(jnp.bfloat16)

    parts = [None] * NZ
    a = b = chunk
    for step in range(1, NZ // 2):
        na = lax.ppermute(a, "z", up)
        nb = lax.ppermute(b, "z", down)
        if step == 1:
            parts[0] = ladder_of(chunk)
        else:
            parts[NZ - step + 1] = ladder_of(a)
            parts[step - 1] = ladder_of(b)
        a, b = na, nb
    half = NY * rows // 2
    fa = lax.ppermute(a[:half], "z", up)
    fb = lax.ppermute(b[half:], "z", down)
    parts[NZ - NZ // 2 + 1] = ladder_of(a)
    parts[NZ // 2 - 1] = ladder_of(b)
    parts[NZ // 2] = jnp.concatenate([ladder_of(fa), ladder_of(fb)], 0)
    rel = jnp.stack([q.reshape(NY, rows, cols) for q in parts], 1)
    rel = jnp.roll(rel, z, axis=1)
    ladder = rel.reshape(NY * NZ * rows, cols)

    blocks = ladder.reshape(OCC, NP, OCC, cols)
    swapped = lax.all_to_all(blocks, PAIR, split_axis=1, concat_axis=1, tiled=True)
    result = blocks.astype(jnp.float32) - jnp.transpose(swapped, (2, 1, 0, 3)).astype(jnp.float32)
    return result.astype(jnp.bfloat16).reshape(NY * NZ * rows, cols)


def solution(mesh):
    fine = Mesh(mesh.devices.reshape(8, 2, 2, NY, NZ), AXES)
    placed = (P(AXES, None), P(None, VIRT), P(), P())
    return jax.shard_map(
        body, mesh=fine, in_specs=placed, out_specs=P(PAIR, VIRT), check_vma=False
    )
```

```python
import jax
import jax.numpy as jnp
import numpy as np
from jax import lax
from jax.sharding import Mesh, PartitionSpec as P

TP = 1024
OCC = 6
NY = 4
NZ = 8
NP = 32
AXES = ("x", "yh", "core", "y", "z")
PAIR = ("x", "yh", "core")
VIRT = ("y", "z")
HALF = OCC // 2
PER = OCC * HALF
PAD = 24
LANES = 128


def one_hot(width, spots):
    out = np.zeros((len(spots), width), np.float32)
    out[np.arange(len(spots)), spots] = 1.0
    return out


def slot(il, q, m):
    c = NP * il + q
    return PAD * (c // OCC) + (c % OCC) * HALF + m


def tables():
    send = np.zeros((NP * PAD, NP * PAD), np.float32)
    for q in range(NP):
        for il in range(OCC):
            for m in range(HALF):
                send[PAD * q + il * HALF + m, slot(il, q, m)] = 1.0
    order = [(il, q, m) for il in range(OCC) for q in range(NP) for m in range(HALF)]
    own = one_hot(NP * PAD, [slot(*o) for o in order])
    mirror = np.stack(
        [
            one_hot(
                NP * PAD,
                [PAD * q + (2 * m + (il + rh) % 2) * HALF + il // 2 for il, q, m in order],
            )
            for rh in range(2)
        ]
    )
    place = np.zeros((OCC, NP * OCC, 2 * NP * HALF), np.float32)
    for il in range(OCC):
        for q in range(NP):
            for jl in range(OCC):
                rh = (il + jl) % 2
                place[il, q * OCC + jl, rh * NP * HALF + q * HALF + jl // 2] = 1.0
    blocks = one_hot(NP, [q for _, q, _ in order])
    return send, own, mirror, place, blocks


SEND, OWN, MIRROR, PLACE, BLOCKS = tables()


def dot(a, b):
    return jnp.dot(a, b, preferred_element_type=jnp.float32)


def body(amplitudes, integrals, amp_pattern, int_pattern):
    rows, kcd = amplitudes.shape
    cols = integrals.shape[1]
    bf = jnp.bfloat16
    p = lax.axis_index(PAIR)
    v = lax.axis_index(VIRT)
    y = lax.axis_index("y")
    z = lax.axis_index("z")
    width = kcd // NZ

    n = jnp.arange(2 * PAD)
    rh, n = n // PAD, n % PAD
    k, m = n // HALF, n % HALF
    il = (OCC * v + k) // NP
    source = jnp.where(n < PER, k * OCC + 2 * m + (il + rh) % 2, -1)
    pick = (source[:, None] == jnp.arange(rows)[None, :]).astype(bf)
    split = dot(pick, amplitudes).astype(bf)
    first = (
        split.reshape(2, PAD, NZ, 2, LANES).transpose(0, 3, 2, 1, 4).reshape(NP, PAD, LANES)
    )
    held = lax.all_to_all(first, VIRT, split_axis=0, concat_axis=0, tiled=True)
    held = held.reshape(NP * PAD, LANES)

    second = dot(jnp.asarray(SEND, bf), held).astype(bf).reshape(NP, PAD, LANES)
    other = lax.all_to_all(second, PAIR, split_axis=0, concat_axis=0, tiled=True)
    other = other.reshape(NP * PAD, LANES)

    pattern = lax.dynamic_index_in_dim(
        amp_pattern, z * width // TP, 2, keepdims=False
    ).astype(jnp.float32)
    mine = lax.dynamic_index_in_dim(pattern, p, 0, keepdims=False)
    theirs = lax.dynamic_index_in_dim(pattern, p, 1, keepdims=False)
    masks = dot(jnp.asarray(BLOCKS, bf), jnp.stack([mine, theirs], 1).astype(bf))
    mirror = lax.dynamic_index_in_dim(jnp.asarray(MIRROR, bf), y // 2, 0, keepdims=False)
    diff = dot(jnp.asarray(OWN, bf), held) * masks[:, :1] - dot(mirror, other) * masks[:, 1:]
    diff = diff.astype(bf)

    gathered = lax.all_gather(diff, "y", axis=0, tiled=False)
    gathered = (
        gathered.reshape(2, 2, OCC, NP * HALF, LANES)
        .transpose(2, 0, 3, 1, 4)
        .reshape(OCC, NP * OCC, width)
    )
    chunk = (
        jnp.einsum(
            "bij,bjk->bik", jnp.asarray(PLACE, bf), gathered, preferred_element_type=jnp.float32
        )
        .astype(bf)
        .reshape(OCC * NP * OCC, width)
    )

    col_mask = lax.dynamic_index_in_dim(int_pattern, v * cols // TP, 1, keepdims=False)
    weighted = integrals * jnp.repeat(col_mask, TP).astype(bf)[:, None]

    def term(c, distance):
        start = lax.rem(z + distance, NZ) * width
        return dot(c, lax.dynamic_slice_in_dim(weighted, start, width, 0))

    up = [(i, (i + 1) % NZ) for i in range(NZ)]
    down = [(i, (i - 1) % NZ) for i in range(NZ)]
    total = None
    a = b = chunk
    for step in range(1, NZ // 2):
        na = lax.ppermute(a, "z", up)
        nb = lax.ppermute(b, "z", down)
        if step == 1:
            total = term(chunk, 0)
        else:
            total = total + term(a, NZ - step + 1) + term(b, step - 1)
        a, b = na, nb
    half = chunk.shape[0] // 2
    fa = lax.ppermute(a[:half], "z", up)
    fb = lax.ppermute(b[half:], "z", down)
    total = total + term(a, NZ - NZ // 2 + 1) + term(b, NZ // 2 - 1)
    low = total[:half] + term(fa, NZ // 2)
    high = total[half:] + term(fb, NZ // 2)
    return jnp.concatenate([low.astype(bf), high.astype(bf)], 0)


def solution(mesh):
    fine = Mesh(mesh.devices.reshape(8, 2, 2, NY, NZ), AXES)
    placed = (P(AXES, None), P(None, VIRT), P(), P())
    return jax.shard_map(
        body, mesh=fine, in_specs=placed, out_specs=P(PAIR, VIRT), check_vma=False
    )
```

```python
import jax
import jax.numpy as jnp
import numpy as np
from jax import lax
from jax.sharding import Mesh, PartitionSpec as P

TP = 1024
OCC = 6
NY = 4
NZ = 8
NP = 32
AXES = ("x", "yh", "core", "y", "z")
PAIR = ("x", "yh", "core")
VIRT = ("y", "z")
HALF = OCC // 2
PER = OCC * HALF
PAD = 24
LANES = 128


def one_hot(width, spots):
    out = np.zeros((len(spots), width), np.float32)
    out[np.arange(len(spots)), spots] = 1.0
    return out


def slot(il, q, m):
    c = NP * il + q
    return PAD * (c // OCC) + (c % OCC) * HALF + m


def tables():
    send = np.zeros((NP * PAD, NP * PAD), np.float32)
    for q in range(NP):
        for il in range(OCC):
            for m in range(HALF):
                send[PAD * q + il * HALF + m, slot(il, q, m)] = 1.0
    order = [(il, q, m) for il in range(OCC) for q in range(NP) for m in range(HALF)]
    own = one_hot(NP * PAD, [slot(*o) for o in order])
    mirror = np.stack(
        [
            one_hot(
                NP * PAD,
                [PAD * q + (2 * m + (il + rh) % 2) * HALF + il // 2 for il, q, m in order],
            )
            for rh in range(2)
        ]
    )
    place = np.zeros((2, OCC, NP * OCC, 2 * NP * HALF), np.float32)
    for rh in range(2):
        for il in range(OCC):
            for q in range(NP):
                for jl in range(OCC):
                    part = (il + jl + rh) % 2
                    place[rh, il, q * OCC + jl, part * NP * HALF + q * HALF + jl // 2] = 1.0
    blocks = one_hot(NP, [q for _, q, _ in order])
    return send, own, mirror, place, blocks


SEND, OWN, MIRROR, PLACE, BLOCKS = tables()


def dot(a, b):
    return jnp.dot(a, b, preferred_element_type=jnp.float32)


def body(amplitudes, integrals, amp_pattern, int_pattern):
    rows, kcd = amplitudes.shape
    cols = integrals.shape[1]
    bf = jnp.bfloat16
    p = lax.axis_index(PAIR)
    v = lax.axis_index(VIRT)
    y = lax.axis_index("y")
    z = lax.axis_index("z")
    width = kcd // NZ

    n = jnp.arange(2 * PAD)
    rh, n = n // PAD, n % PAD
    k, m = n // HALF, n % HALF
    il = (OCC * v + k) // NP
    source = jnp.where(n < PER, k * OCC + 2 * m + (il + rh) % 2, -1)
    pick = (source[:, None] == jnp.arange(rows)[None, :]).astype(bf)
    split = dot(pick, amplitudes).astype(bf)
    first = (
        split.reshape(2, PAD, NZ, 2, LANES).transpose(0, 3, 2, 1, 4).reshape(NP, PAD, LANES)
    )
    held = lax.all_to_all(first, VIRT, split_axis=0, concat_axis=0, tiled=True)
    held = held.reshape(NP * PAD, LANES)

    second = dot(jnp.asarray(SEND, bf), held).astype(bf).reshape(NP, PAD, LANES)
    other = lax.all_to_all(second, PAIR, split_axis=0, concat_axis=0, tiled=True)
    other = other.reshape(NP * PAD, LANES)

    pattern = lax.dynamic_index_in_dim(
        amp_pattern, z * width // TP, 2, keepdims=False
    ).astype(jnp.float32)
    mine = lax.dynamic_index_in_dim(pattern, p, 0, keepdims=False)
    theirs = lax.dynamic_index_in_dim(pattern, p, 1, keepdims=False)
    masks = dot(jnp.asarray(BLOCKS, bf), jnp.stack([mine, theirs], 1).astype(bf))
    mirror = lax.dynamic_index_in_dim(jnp.asarray(MIRROR, bf), y // 2, 0, keepdims=False)
    diff = dot(jnp.asarray(OWN, bf), held) * masks[:, :1] - dot(mirror, other) * masks[:, 1:]
    diff = diff.astype(bf)

    col_mask = lax.dynamic_index_in_dim(int_pattern, v * cols // TP, 1, keepdims=False)
    weighted = integrals * jnp.repeat(col_mask, TP).astype(bf)[:, None]
    weighted = weighted.reshape(NZ, 2, LANES, cols)
    weighted = jnp.where(y % 2 == 0, weighted, weighted[:, ::-1]).reshape(kcd, cols)
    core = lax.axis_index("core")
    sign = 1 - 2 * core

    def term(c, distance):
        start = lax.rem(z + sign * distance + NZ, NZ) * width
        return dot(c, lax.dynamic_slice_in_dim(weighted, start, width, 0))

    near = lax.ppermute(diff, "y", [(i, i ^ 1) for i in range(NY)])
    piece = jnp.concatenate([diff, near], 1)
    pieces = [piece, lax.ppermute(piece, "y", [(i, i ^ 2) for i in range(NY)])]

    def shift(step):
        return [
            (c * NZ + i, c * NZ + (i + (1 - 2 * c) * step) % NZ)
            for c in range(2)
            for i in range(NZ)
        ]

    ways = (shift(1), shift(-1))
    front = [list(pieces), list(pieces)]
    totals = [None, None]
    for step in range(1, NZ // 2 + 1):
        for i in range(2):
            last = step == NZ // 2
            if totals[i] is None:
                totals[i] = term(pieces[i], 0)
            for w in range(2):
                if last and w != i:
                    continue
                front[w][i] = lax.ppermute(front[w][i], ("core", "z"), ways[w])
                totals[i] = totals[i] + term(front[w][i], -step if w == 0 else step)
    both = jnp.concatenate(
        [t.astype(bf).reshape(OCC, NP * HALF, cols) for t in totals], 1
    )
    place = lax.dynamic_index_in_dim(jnp.asarray(PLACE, bf), y // 2, 0, keepdims=False)
    out = jnp.einsum("bij,bjk->bik", place, both, preferred_element_type=jnp.float32)
    return out.astype(bf).reshape(OCC * NP * OCC, cols)


def solution(mesh):
    fine = Mesh(mesh.devices.reshape(8, 2, 2, NY, NZ), AXES)
    placed = (P(AXES, None), P(None, VIRT), P(), P())
    return jax.shard_map(
        body, mesh=fine, in_specs=placed, out_specs=P(PAIR, VIRT), check_vma=False
    )
```

```python
import jax
import jax.numpy as jnp
import numpy as np
from jax import lax
from jax.sharding import Mesh, PartitionSpec as P

TP = 1024
OCC = 6
NY = 4
NZ = 8
NP = 32
AXES = ("x", "yh", "core", "y", "z")
PAIR = ("x", "yh", "core")
VIRT = ("y", "z")
HALF = OCC // 2
PER = OCC * HALF
PAD = 24
LANES = 128


def one_hot(width, spots):
    out = np.zeros((len(spots), width), np.float32)
    out[np.arange(len(spots)), spots] = 1.0
    return out


def slot(il, q, m):
    c = NP * il + q
    return PAD * (c // OCC) + (c % OCC) * HALF + m


def tables():
    send = np.zeros((NP * PAD, NP * PAD), np.float32)
    for q in range(NP):
        for il in range(OCC):
            for m in range(HALF):
                send[PAD * q + il * HALF + m, slot(il, q, m)] = 1.0
    order = [(il, q, m) for il in range(OCC) for q in range(NP) for m in range(HALF)]
    own = one_hot(NP * PAD, [slot(*o) for o in order])
    mirror = np.stack(
        [
            one_hot(
                NP * PAD,
                [PAD * q + (2 * m + (il + rh) % 2) * HALF + il // 2 for il, q, m in order],
            )
            for rh in range(2)
        ]
    )
    place = np.zeros((OCC, NP * OCC, 2 * NP * HALF), np.float32)
    for il in range(OCC):
        for q in range(NP):
            for jl in range(OCC):
                rh = (il + jl) % 2
                place[il, q * OCC + jl, rh * NP * HALF + q * HALF + jl // 2] = 1.0
    blocks = one_hot(NP, [q for _, q, _ in order])
    return send, own, mirror, place, blocks


SEND, OWN, MIRROR, PLACE, BLOCKS = tables()


def dot(a, b):
    return jnp.dot(a, b, preferred_element_type=jnp.float32)


def body(amplitudes, integrals, amp_pattern, int_pattern):
    rows, kcd = amplitudes.shape
    cols = integrals.shape[1]
    bf = jnp.bfloat16
    p = lax.axis_index(PAIR)
    v = lax.axis_index(VIRT)
    y = lax.axis_index("y")
    z = lax.axis_index("z")
    width = kcd // NZ

    n = jnp.arange(2 * PAD)
    rh, n = n // PAD, n % PAD
    k, m = n // HALF, n % HALF
    il = (OCC * v + k) // NP
    source = jnp.where(n < PER, k * OCC + 2 * m + (il + rh) % 2, -1)
    pick = (source[:, None] == jnp.arange(rows)[None, :]).astype(bf)
    split = dot(pick, amplitudes).astype(bf)
    first = (
        split.reshape(2, PAD, NZ, 2, LANES).transpose(0, 3, 2, 1, 4).reshape(NP, PAD, LANES)
    )
    held = lax.all_to_all(first, VIRT, split_axis=0, concat_axis=0, tiled=True)
    held = held.reshape(NP * PAD, LANES)

    second = dot(jnp.asarray(SEND, bf), held).astype(bf).reshape(NP, PAD, LANES)
    other = lax.all_to_all(second, PAIR, split_axis=0, concat_axis=0, tiled=True)
    other = other.reshape(NP * PAD, LANES)

    pattern = lax.dynamic_index_in_dim(
        amp_pattern, z * width // TP, 2, keepdims=False
    ).astype(jnp.float32)
    mine = lax.dynamic_index_in_dim(pattern, p, 0, keepdims=False)
    theirs = lax.dynamic_index_in_dim(pattern, p, 1, keepdims=False)
    masks = dot(jnp.asarray(BLOCKS, bf), jnp.stack([mine, theirs], 1).astype(bf))
    mirror = lax.dynamic_index_in_dim(jnp.asarray(MIRROR, bf), y // 2, 0, keepdims=False)
    diff = dot(jnp.asarray(OWN, bf), held) * masks[:, :1] - dot(mirror, other) * masks[:, 1:]
    diff = diff.astype(bf)

    gathered = lax.all_gather(diff, "y", axis=0, tiled=False)
    pieces = [jnp.concatenate([gathered[2 * r], gathered[2 * r + 1]], 1) for r in range(2)]

    col_mask = lax.dynamic_index_in_dim(int_pattern, v * cols // TP, 1, keepdims=False)
    weighted = integrals * jnp.repeat(col_mask, TP).astype(bf)[:, None]

    sign = 1 - 2 * lax.axis_index("core")

    def term(c, distance):
        start = lax.rem(z + sign * distance + NZ, NZ) * width
        return dot(c, lax.dynamic_slice_in_dim(weighted, start, width, 0))

    def shift(step):
        return [
            (c * NZ + i, c * NZ + (i + (1 - 2 * c) * step) % NZ)
            for c in range(2)
            for i in range(NZ)
        ]

    ways = (shift(1), shift(-1))
    front = [list(pieces), list(pieces)]
    totals = [term(c, 0) for c in pieces]
    for step in range(1, NZ // 2 + 1):
        for i in range(2):
            for w in range(2):
                if step == NZ // 2 and w != i:
                    continue
                front[w][i] = lax.ppermute(front[w][i], ("core", "z"), ways[w])
                totals[i] = totals[i] + term(front[w][i], -step if w == 0 else step)
    both = jnp.concatenate([t.astype(bf).reshape(OCC, NP * HALF, cols) for t in totals], 1)
    out = jnp.einsum(
        "bij,bjk->bik", jnp.asarray(PLACE, bf), both, preferred_element_type=jnp.float32
    )
    return out.astype(bf).reshape(OCC * NP * OCC, cols)


def solution(mesh):
    fine = Mesh(mesh.devices.reshape(8, 2, 2, NY, NZ), AXES)
    placed = (P(AXES, None), P(None, VIRT), P(), P())
    return jax.shard_map(
        body, mesh=fine, in_specs=placed, out_specs=P(PAIR, VIRT), check_vma=False
    )
```

```python
import jax
import jax.numpy as jnp
import numpy as np
from jax import lax
from jax.experimental import pallas as pl
from jax.experimental.pallas import tpu as pltpu
from jax.sharding import Mesh, PartitionSpec as P

TP = 1024
OCC = 6
NY = 4
NZ = 8
NP = 32
AXES = ("x", "yh", "core", "y", "z")
PAIR = ("x", "yh", "core")
VIRT = ("y", "z")
HALF = OCC // 2
PER = OCC * HALF
PAD = 24
LANES = 128


def one_hot(width, spots):
    out = np.zeros((len(spots), width), np.float32)
    out[np.arange(len(spots)), spots] = 1.0
    return out


def slot(il, q, m):
    c = NP * il + q
    return PAD * (c // OCC) + (c % OCC) * HALF + m


def tables():
    send = np.zeros((NP * PAD, NP * PAD), np.float32)
    for q in range(NP):
        for il in range(OCC):
            for m in range(HALF):
                send[PAD * q + il * HALF + m, slot(il, q, m)] = 1.0
    order = [(il, q, m) for il in range(OCC) for q in range(NP) for m in range(HALF)]
    own = one_hot(NP * PAD, [slot(*o) for o in order])
    mirror = np.stack(
        [
            one_hot(
                NP * PAD,
                [PAD * q + (2 * m + (il + rh) % 2) * HALF + il // 2 for il, q, m in order],
            )
            for rh in range(2)
        ]
    )
    place = np.array(
        [
            [((il + jl) % 2 * NP + q) * HALF + jl // 2 for q in range(NP) for jl in range(OCC)]
            for il in range(OCC)
        ],
        np.int32,
    )
    blocks = one_hot(NP, [q for _, q, _ in order])
    return send, own, mirror, place, blocks


SEND, OWN, MIRROR, PLACE, BLOCKS = tables()


def dot(a, b):
    return jnp.dot(a, b, preferred_element_type=jnp.float32)


TILE = 192


def terms_kernel(starts_ref, weights_ref, *refs):
    count = (len(refs) - 2) // 2
    width = refs[0].shape[1]
    for i in range(2):
        chunks = refs[i * count : (i + 1) * count]
        out = refs[2 * count + i]

        def tile(t, carry, chunks=chunks, out=out):
            rows = pl.ds(pl.multiple_of(t * TILE, TILE), TILE)
            total = None
            for j, chunk in enumerate(chunks):
                here = pl.ds(pl.multiple_of(starts_ref[j], width), width)
                part = jnp.dot(
                    chunk[rows, :], weights_ref[here, :], preferred_element_type=jnp.float32
                )
                total = part if total is None else total + part
            out[rows, :] = total
            return carry

        lax.fori_loop(0, out.shape[0] // TILE, tile, 0)


def terms(starts, weights, chunks):
    rows, width = chunks[0][0].shape
    cols = weights.shape[1]
    count = len(chunks[0])
    out = jax.ShapeDtypeStruct((rows, cols), jnp.float32)
    vmem = pl.BlockSpec(memory_space=pltpu.VMEM)
    return pl.pallas_call(
        terms_kernel,
        out_shape=(out, out),
        in_specs=[pl.BlockSpec(memory_space=pltpu.SMEM)] + [vmem] * (1 + 2 * count),
        out_specs=(vmem, vmem),
        compiler_params=pltpu.CompilerParams(vmem_limit_bytes=32 * 2**20),
        cost_estimate=pl.CostEstimate(
            flops=4 * count * rows * width * cols,
            bytes_accessed=2 * weights.size + 4 * count * rows * width + 8 * rows * cols,
            transcendentals=0,
        ),
    )(starts, weights, *chunks[0], *chunks[1])


def body(amplitudes, integrals, amp_pattern, int_pattern):
    rows, kcd = amplitudes.shape
    cols = integrals.shape[1]
    bf = jnp.bfloat16
    p = lax.axis_index(PAIR)
    v = lax.axis_index(VIRT)
    y = lax.axis_index("y")
    z = lax.axis_index("z")
    width = kcd // NZ

    n = jnp.arange(2 * PAD)
    rh, n = n // PAD, n % PAD
    k, m = n // HALF, n % HALF
    il = (OCC * v + k) // NP
    source = jnp.where(n < PER, k * OCC + 2 * m + (il + rh) % 2, -1)
    pick = (source[:, None] == jnp.arange(rows)[None, :]).astype(bf)
    split = dot(pick, amplitudes).astype(bf)
    first = (
        split.reshape(2, PAD, NZ, 2, LANES).transpose(0, 3, 2, 1, 4).reshape(NP, PAD, LANES)
    )
    held = lax.all_to_all(first, VIRT, split_axis=0, concat_axis=0, tiled=True)
    held = held.reshape(NP * PAD, LANES)

    second = dot(jnp.asarray(SEND, bf), held).astype(bf).reshape(NP, PAD, LANES)
    other = lax.all_to_all(second, PAIR, split_axis=0, concat_axis=0, tiled=True)
    other = other.reshape(NP * PAD, LANES)

    pattern = lax.dynamic_index_in_dim(
        amp_pattern, z * width // TP, 2, keepdims=False
    ).astype(jnp.float32)
    mine = lax.dynamic_index_in_dim(pattern, p, 0, keepdims=False)
    theirs = lax.dynamic_index_in_dim(pattern, p, 1, keepdims=False)
    masks = dot(jnp.asarray(BLOCKS, bf), jnp.stack([mine, theirs], 1).astype(bf))
    mirror = lax.dynamic_index_in_dim(jnp.asarray(MIRROR, bf), y // 2, 0, keepdims=False)
    diff = dot(jnp.asarray(OWN, bf), held) * masks[:, :1] - dot(mirror, other) * masks[:, 1:]
    diff = diff.astype(bf)

    gathered = lax.all_gather(diff, "y", axis=0, tiled=False)
    pieces = [jnp.concatenate([gathered[2 * r], gathered[2 * r + 1]], 1) for r in range(2)]

    col_mask = lax.dynamic_index_in_dim(int_pattern, v * cols // TP, 1, keepdims=False)
    weighted = integrals * jnp.repeat(col_mask, TP).astype(bf)[:, None]

    place = (jnp.asarray(PLACE)[:, :, None] == jnp.arange(NP * OCC)[None, None, :]).astype(bf)
    weighted, place = lax.optimization_barrier((weighted, place))
    sign = 1 - 2 * lax.axis_index("core")

    def term(c, distance):
        start = lax.rem(z + sign * distance + NZ, NZ) * width
        return dot(c, lax.dynamic_slice_in_dim(weighted, start, width, 0))

    def shift(step):
        return [
            (c * NZ + i, c * NZ + (i + (1 - 2 * c) * step) % NZ)
            for c in range(2)
            for i in range(NZ)
        ]

    ways = (shift(1), shift(-1))
    front = [list(pieces), list(pieces)]
    held = [[(c, 0)] for c in pieces]
    for step in range(1, NZ // 2):
        for i in range(2):
            for w in range(2):
                front[w][i] = lax.ppermute(front[w][i], ("core", "z"), ways[w])
                held[i].append((front[w][i], -step if w == 0 else step))
    sent = [lax.ppermute(front[i][i], ("core", "z"), ways[i]) for i in range(2)]
    starts = jnp.stack([lax.rem(z + sign * d + NZ, NZ) * width for _, d in held[0]])
    sums = terms(starts.astype(jnp.int32), weighted, [[c for c, _ in h] for h in held])
    totals = [sums[i] + term(sent[i], NZ // 2) for i in range(2)]
    both = jnp.concatenate([t.astype(bf).reshape(OCC, NP * HALF, cols) for t in totals], 1)
    out = jnp.einsum(
        "bij,bjk->bik", place, both, preferred_element_type=jnp.float32
    )
    return out.astype(bf).reshape(OCC * NP * OCC, cols)


def solution(mesh):
    fine = Mesh(mesh.devices.reshape(8, 2, 2, NY, NZ), AXES)
    placed = (P(AXES, None), P(None, VIRT), P(), P())
    return jax.shard_map(
        body, mesh=fine, in_specs=placed, out_specs=P(PAIR, VIRT), check_vma=False
    )
```

```python
import jax
import jax.numpy as jnp
import numpy as np
from jax import lax
from jax.sharding import Mesh, PartitionSpec as P

TP = 1024
OCC = 6
NY = 4
NZ = 8
NP = 32
AXES = ("x", "yh", "core", "y", "z")
PAIR = ("x", "yh", "core")
VIRT = ("y", "z")
HALF = OCC // 2
PER = OCC * HALF
PAD = 24
LANES = 128


def one_hot(width, spots):
    out = np.zeros((len(spots), width), np.float32)
    out[np.arange(len(spots)), spots] = 1.0
    return out


def slot(il, q, m):
    c = NP * il + q
    return PAD * (c // OCC) + (c % OCC) * HALF + m


def tables():
    send = np.zeros((NP * PAD, NP * PAD), np.float32)
    for q in range(NP):
        for il in range(OCC):
            for m in range(HALF):
                send[PAD * q + il * HALF + m, slot(il, q, m)] = 1.0
    order = [(il, q, m) for il in range(OCC) for q in range(NP) for m in range(HALF)]
    own = one_hot(NP * PAD, [slot(*o) for o in order])
    mirror = np.stack(
        [
            one_hot(
                NP * PAD,
                [PAD * q + (2 * m + (il + rh) % 2) * HALF + il // 2 for il, q, m in order],
            )
            for rh in range(2)
        ]
    )
    place = np.zeros((OCC, NP * OCC, 2 * NP * HALF), np.float32)
    for il in range(OCC):
        for q in range(NP):
            for jl in range(OCC):
                rh = (il + jl) % 2
                place[il, q * OCC + jl, rh * NP * HALF + q * HALF + jl // 2] = 1.0
    blocks = one_hot(NP, [q for _, q, _ in order])
    return send, own, mirror, place, blocks


SEND, OWN, MIRROR, PLACE, BLOCKS = tables()


def dot(a, b):
    return jnp.dot(a, b, preferred_element_type=jnp.float32)


def body(amplitudes, integrals, amp_pattern, int_pattern):
    rows, kcd = amplitudes.shape
    cols = integrals.shape[1]
    bf = jnp.bfloat16
    p = lax.axis_index(PAIR)
    v = lax.axis_index(VIRT)
    y = lax.axis_index("y")
    z = lax.axis_index("z")
    width = kcd // NZ

    n = jnp.arange(2 * PAD)
    rh, n = n // PAD, n % PAD
    k, m = n // HALF, n % HALF
    il = (OCC * v + k) // NP
    source = jnp.where(n < PER, k * OCC + 2 * m + (il + rh) % 2, -1)
    pick = (source[:, None] == jnp.arange(rows)[None, :]).astype(bf)
    split = dot(pick, amplitudes).astype(bf)
    first = (
        split.reshape(2, PAD, NZ, 2, LANES).transpose(0, 3, 2, 1, 4).reshape(NP, PAD, LANES)
    )
    held = lax.all_to_all(first, VIRT, split_axis=0, concat_axis=0, tiled=True)
    held = held.reshape(NP * PAD, LANES)

    second = dot(jnp.asarray(SEND, bf), held).astype(bf).reshape(NP, PAD, LANES)
    other = lax.all_to_all(second, PAIR, split_axis=0, concat_axis=0, tiled=True)
    other = other.reshape(NP * PAD, LANES)

    pattern = lax.dynamic_index_in_dim(
        amp_pattern, z * width // TP, 2, keepdims=False
    ).astype(jnp.float32)
    mine = lax.dynamic_index_in_dim(pattern, p, 0, keepdims=False)
    theirs = lax.dynamic_index_in_dim(pattern, p, 1, keepdims=False)
    masks = dot(jnp.asarray(BLOCKS, bf), jnp.stack([mine, theirs], 1).astype(bf))
    mirror = lax.dynamic_index_in_dim(jnp.asarray(MIRROR, bf), y // 2, 0, keepdims=False)
    diff = dot(jnp.asarray(OWN, bf), held) * masks[:, :1] - dot(mirror, other) * masks[:, 1:]
    diff = diff.astype(bf)

    gathered = lax.all_gather(diff, "y", axis=0, tiled=False)
    gathered = gathered.reshape(2, 2, NP * PER, LANES)
    e = y % 2
    mine = lax.dynamic_index_in_dim(gathered, e, 1, keepdims=False).reshape(-1, LANES)
    pair = lax.dynamic_index_in_dim(gathered, 1 - e, 1, keepdims=False).reshape(-1, LANES)

    col_mask = lax.dynamic_index_in_dim(int_pattern, v * cols // TP, 1, keepdims=False)
    weighted = integrals * jnp.repeat(col_mask, TP).astype(bf)[:, None]

    sign = 1 - 2 * lax.axis_index("core")

    def term(c, distance, half):
        start = lax.rem(z + sign * distance + NZ, NZ) * width + half * LANES
        return dot(c, lax.dynamic_slice_in_dim(weighted, start, LANES, 0))

    def shift(step):
        return [
            (c * NZ + i, c * NZ + (i + (1 - 2 * c) * step) % NZ)
            for c in range(2)
            for i in range(NZ)
        ]

    ways = (shift(1), shift(-1))
    def hop(c, w):
        return lax.ppermute(c, ("core", "z"), ways[w])

    def across(c):
        return lax.ppermute(c, "y", [(i, i ^ 1) for i in range(NY)])

    front, other = [mine, mine], [pair, pair]
    total = term(mine, 0, e) + term(pair, 0, 1 - e)
    for step in range(1, 4):
        for w in range(2):
            d = -step if w == 0 else step
            front[w] = hop(front[w], w)
            total = total + term(front[w], d, e)
            if step < 3:
                ready = other[w]
                if step == 2:
                    ready, _ = lax.optimization_barrier((ready, front[w]))
                other[w] = hop(ready, w)
            else:
                other[w] = across(front[w])
            total = total + term(other[w], d, 1 - e)
    far = hop(front[0], 0)
    total = total + term(far, NZ // 2, e) + term(across(far), NZ // 2, 1 - e)
    both = (
        total.astype(bf).reshape(2, OCC, NP * HALF, cols).transpose(1, 0, 2, 3)
    ).reshape(OCC, NP * OCC, cols)
    out = jnp.einsum(
        "bij,bjk->bik", jnp.asarray(PLACE, bf), both, preferred_element_type=jnp.float32
    )
    return out.astype(bf).reshape(OCC * NP * OCC, cols)


def solution(mesh):
    fine = Mesh(mesh.devices.reshape(8, 2, 2, NY, NZ), AXES)
    placed = (P(AXES, None), P(None, VIRT), P(), P())
    return jax.shard_map(
        body, mesh=fine, in_specs=placed, out_specs=P(PAIR, VIRT), check_vma=False
    )
```

```python
import jax
import jax.numpy as jnp
import numpy as np
from jax import lax
from jax.sharding import Mesh, PartitionSpec as P

TP = 1024
OCC = 6
NY = 4
NZ = 8
NP = 32
AXES = ("x", "yh", "core", "y", "z")
PAIR = ("x", "yh", "core")
VIRT = ("y", "z")
HALF = OCC // 2
PER = OCC * HALF
PAD = 24
LANES = 128


def one_hot(width, spots):
    out = np.zeros((len(spots), width), np.float32)
    out[np.arange(len(spots)), spots] = 1.0
    return out


def slot(il, q, m):
    c = NP * il + q
    return PAD * (c // OCC) + (c % OCC) * HALF + m


def tables():
    send = np.zeros((NP * PAD, NP * PAD), np.float32)
    for q in range(NP):
        for il in range(OCC):
            for m in range(HALF):
                send[PAD * q + il * HALF + m, slot(il, q, m)] = 1.0
    order = [(il, q, m) for il in range(OCC) for q in range(NP) for m in range(HALF)]
    own = one_hot(NP * PAD, [slot(*o) for o in order])
    mirror = np.stack(
        [
            one_hot(
                NP * PAD,
                [PAD * q + (2 * m + (il + rh) % 2) * HALF + il // 2 for il, q, m in order],
            )
            for rh in range(2)
        ]
    )
    place = np.zeros((OCC, NP * OCC, 2 * NP * HALF), np.float32)
    for il in range(OCC):
        for q in range(NP):
            for jl in range(OCC):
                rh = (il + jl) % 2
                place[il, q * OCC + jl, rh * NP * HALF + q * HALF + jl // 2] = 1.0
    blocks = one_hot(NP, [q for _, q, _ in order])
    return send, own, mirror, place, blocks


SEND, OWN, MIRROR, PLACE, BLOCKS = tables()


def dot(a, b):
    return jnp.dot(a, b, preferred_element_type=jnp.float32)


def body(amplitudes, integrals, amp_pattern, int_pattern):
    rows, kcd = amplitudes.shape
    cols = integrals.shape[1]
    bf = jnp.bfloat16
    p = lax.axis_index(PAIR)
    v = lax.axis_index(VIRT)
    y = lax.axis_index("y")
    z = lax.axis_index("z")
    width = kcd // NZ

    n = jnp.arange(2 * PAD)
    rh, n = n // PAD, n % PAD
    k, m = n // HALF, n % HALF
    il = (OCC * v + k) // NP
    source = jnp.where(n < PER, k * OCC + 2 * m + (il + rh) % 2, -1)
    pick = (source[:, None] == jnp.arange(rows)[None, :]).astype(bf)
    split = dot(pick, amplitudes).astype(bf)
    first = (
        split.reshape(2, PAD, NZ, 2, LANES).transpose(0, 3, 2, 1, 4).reshape(NP, PAD, LANES)
    )
    held = lax.all_to_all(first, VIRT, split_axis=0, concat_axis=0, tiled=True)
    held = held.reshape(NP * PAD, LANES)

    second = dot(jnp.asarray(SEND, bf), held).astype(bf).reshape(NP, PAD, LANES)
    other = lax.all_to_all(second, PAIR, split_axis=0, concat_axis=0, tiled=True)
    other = other.reshape(NP * PAD, LANES)

    pattern = lax.dynamic_index_in_dim(
        amp_pattern, z * width // TP, 2, keepdims=False
    ).astype(jnp.float32)
    mine = lax.dynamic_index_in_dim(pattern, p, 0, keepdims=False)
    theirs = lax.dynamic_index_in_dim(pattern, p, 1, keepdims=False)
    masks = dot(jnp.asarray(BLOCKS, bf), jnp.stack([mine, theirs], 1).astype(bf))
    mirror = lax.dynamic_index_in_dim(jnp.asarray(MIRROR, bf), y // 2, 0, keepdims=False)
    diff = dot(jnp.asarray(OWN, bf), held) * masks[:, :1] - dot(mirror, other) * masks[:, 1:]
    diff = diff.astype(bf)

    gathered = lax.all_gather(diff, "y", axis=0, tiled=False)
    gathered = gathered.reshape(2, 2, NP * PER, LANES)
    e = y % 2
    mine = lax.dynamic_index_in_dim(gathered, e, 1, keepdims=False).reshape(-1, LANES)
    pair = lax.dynamic_index_in_dim(gathered, 1 - e, 1, keepdims=False).reshape(-1, LANES)

    col_mask = lax.dynamic_index_in_dim(int_pattern, v * cols // TP, 1, keepdims=False)
    weighted = integrals * jnp.repeat(col_mask, TP).astype(bf)[:, None]

    sign = 1 - 2 * lax.axis_index("core")

    def term(c, distance, half):
        start = lax.rem(z + sign * distance + NZ, NZ) * width + half * LANES
        return dot(c, lax.dynamic_slice_in_dim(weighted, start, LANES, 0))

    def shift(step):
        return [
            (c * NZ + i, c * NZ + (i + (1 - 2 * c) * step) % NZ)
            for c in range(2)
            for i in range(NZ)
        ]

    ways = (shift(1), shift(-1))
    def hop(c, w):
        return lax.ppermute(c, ("core", "z"), ways[w])

    def across(c):
        return lax.ppermute(c, "y", [(i, i ^ 1) for i in range(NY)])

    front, other = [mine, mine], [pair, pair]
    total = term(mine, 0, e) + term(pair, 0, 1 - e)
    for step in range(1, 4):
        for w in range(2):
            d = -step if w == 0 else step
            front[w] = hop(front[w], w)
            total = total + term(front[w], d, e)
            other[w] = across(front[w]) if step == 3 else hop(other[w], w)
            total = total + term(other[w], d, 1 - e)
    far = hop(front[0], 0)
    total = total + term(far, NZ // 2, e) + term(across(far), NZ // 2, 1 - e)
    both = (
        total.astype(bf).reshape(2, OCC, NP * HALF, cols).transpose(1, 0, 2, 3)
    ).reshape(OCC, NP * OCC, cols)
    out = jnp.einsum(
        "bij,bjk->bik", jnp.asarray(PLACE, bf), both, preferred_element_type=jnp.float32
    )
    return out.astype(bf).reshape(OCC * NP * OCC, cols)


def solution(mesh):
    fine = Mesh(mesh.devices.reshape(8, 2, 2, NY, NZ), AXES)
    placed = (P(AXES, None), P(None, VIRT), P(), P())
    return jax.shard_map(
        body, mesh=fine, in_specs=placed, out_specs=P(PAIR, VIRT), check_vma=False
    )
```

```python
import jax
import jax.numpy as jnp
import numpy as np
from jax import lax
from jax.sharding import Mesh, PartitionSpec as P

TP = 1024
OCC = 6
NY = 4
NZ = 8
NP = 32
AXES = ("x", "yh", "core", "y", "z")
PAIR = ("x", "yh", "core")
VIRT = ("y", "z")
HALF = OCC // 2
PER = OCC * HALF
PAD = 24
LANES = 128


def one_hot(width, spots):
    out = np.zeros((len(spots), width), np.float32)
    out[np.arange(len(spots)), spots] = 1.0
    return out


def slot(il, q, m):
    c = NP * il + q
    return PAD * (c // OCC) + (c % OCC) * HALF + m


def tables():
    send = np.zeros((NP * PAD, NP * PAD), np.float32)
    for q in range(NP):
        for il in range(OCC):
            for m in range(HALF):
                send[PAD * q + il * HALF + m, slot(il, q, m)] = 1.0
    order = [(il, q, m) for il in range(OCC) for q in range(NP) for m in range(HALF)]
    own = one_hot(NP * PAD, [slot(*o) for o in order])
    mirror = np.stack(
        [
            one_hot(
                NP * PAD,
                [PAD * q + (2 * m + (il + rh) % 2) * HALF + il // 2 for il, q, m in order],
            )
            for rh in range(2)
        ]
    )
    place = np.zeros((OCC, NP * OCC, 2 * NP * HALF), np.float32)
    for il in range(OCC):
        for q in range(NP):
            for jl in range(OCC):
                rh = (il + jl) % 2
                place[il, q * OCC + jl, rh * NP * HALF + q * HALF + jl // 2] = 1.0
    blocks = one_hot(NP, [q for _, q, _ in order])
    return send, own, mirror, place, blocks


SEND, OWN, MIRROR, PLACE, BLOCKS = tables()


def dot(a, b):
    return jnp.dot(a, b, preferred_element_type=jnp.float32)


def body(amplitudes, integrals, amp_pattern, int_pattern):
    rows, kcd = amplitudes.shape
    cols = integrals.shape[1]
    bf = jnp.bfloat16
    p = lax.axis_index(PAIR)
    v = lax.axis_index(VIRT)
    y = lax.axis_index("y")
    z = lax.axis_index("z")
    width = kcd // NZ

    n = jnp.arange(2 * PAD)
    rh, n = n // PAD, n % PAD
    k, m = n // HALF, n % HALF
    il = (OCC * v + k) // NP
    source = jnp.where(n < PER, k * OCC + 2 * m + (il + rh) % 2, -1)
    pick = (source[:, None] == jnp.arange(rows)[None, :]).astype(bf)
    split = dot(pick, amplitudes).astype(bf)
    first = (
        split.reshape(2, PAD, NZ, 2, LANES).transpose(0, 3, 2, 1, 4).reshape(NP, PAD, LANES)
    )
    held = lax.all_to_all(first, VIRT, split_axis=0, concat_axis=0, tiled=True)
    held = held.reshape(NP * PAD, LANES)

    second = dot(jnp.asarray(SEND, bf), held).astype(bf).reshape(NP, PAD, LANES)
    other = lax.all_to_all(second, PAIR, split_axis=0, concat_axis=0, tiled=True)
    other = other.reshape(NP * PAD, LANES)

    pattern = lax.dynamic_index_in_dim(
        amp_pattern, z * width // TP, 2, keepdims=False
    ).astype(jnp.float32)
    mine = lax.dynamic_index_in_dim(pattern, p, 0, keepdims=False)
    theirs = lax.dynamic_index_in_dim(pattern, p, 1, keepdims=False)
    masks = dot(jnp.asarray(BLOCKS, bf), jnp.stack([mine, theirs], 1).astype(bf))
    mirror = lax.dynamic_index_in_dim(jnp.asarray(MIRROR, bf), y // 2, 0, keepdims=False)
    diff = dot(jnp.asarray(OWN, bf), held) * masks[:, :1] - dot(mirror, other) * masks[:, 1:]
    diff = diff.astype(bf)

    gathered = lax.all_gather(diff, "y", axis=0, tiled=False)
    chunk = jnp.concatenate(
        [jnp.concatenate([gathered[2 * r], gathered[2 * r + 1]], 1) for r in range(2)], 0
    )

    col_mask = lax.dynamic_index_in_dim(int_pattern, v * cols // TP, 1, keepdims=False)
    weighted = integrals * jnp.repeat(col_mask, TP).astype(bf)[:, None]

    sign = 1 - 2 * lax.axis_index("core")

    def term(c, distance):
        start = lax.rem(z + sign * distance + NZ, NZ) * width
        return dot(c, lax.dynamic_slice_in_dim(weighted, start, width, 0))

    def shift(step):
        return [
            (c * NZ + i, c * NZ + (i + (1 - 2 * c) * step) % NZ)
            for c in range(2)
            for i in range(NZ)
        ]

    ways = (shift(1), shift(-1))
    front = [chunk, chunk]
    total = term(chunk, 0)
    for step in range(1, NZ // 2 + 1):
        for w in range(2 if step < NZ // 2 else 1):
            front[w] = lax.ppermute(front[w], ("core", "z"), ways[w])
            total = total + term(front[w], -step if w == 0 else step)
    both = (
        total.astype(bf).reshape(2, OCC, NP * HALF, cols).transpose(1, 0, 2, 3)
    ).reshape(OCC, NP * OCC, cols)
    out = jnp.einsum(
        "bij,bjk->bik", jnp.asarray(PLACE, bf), both, preferred_element_type=jnp.float32
    )
    return out.astype(bf).reshape(OCC * NP * OCC, cols)


def solution(mesh):
    fine = Mesh(mesh.devices.reshape(8, 2, 2, NY, NZ), AXES)
    placed = (P(AXES, None), P(None, VIRT), P(), P())
    return jax.shard_map(
        body, mesh=fine, in_specs=placed, out_specs=P(PAIR, VIRT), check_vma=False
    )
```

```python
import jax
import jax.numpy as jnp
import numpy as np
from jax import lax
from jax.sharding import Mesh, PartitionSpec as P

TP = 1024
OCC = 6
NY = 4
NZ = 8
NP = 32
AXES = ("x", "yh", "core", "y", "z")
PAIR = ("x", "yh", "core")
VIRT = ("y", "z")
HALF = OCC // 2
PER = OCC * HALF
PAD = 24
LANES = 128


def one_hot(width, spots):
    out = np.zeros((len(spots), width), np.float32)
    out[np.arange(len(spots)), spots] = 1.0
    return out


def slot(il, q, m):
    c = NP * il + q
    return PAD * (c // OCC) + (c % OCC) * HALF + m


def tables():
    send = np.zeros((NP * PAD, NP * PAD), np.float32)
    for q in range(NP):
        for il in range(OCC):
            for m in range(HALF):
                send[PAD * q + il * HALF + m, slot(il, q, m)] = 1.0
    order = [(il, q, m) for il in range(OCC) for q in range(NP) for m in range(HALF)]
    own = one_hot(NP * PAD, [slot(*o) for o in order])
    mirror = np.stack(
        [
            one_hot(
                NP * PAD,
                [PAD * q + (2 * m + (il + rh) % 2) * HALF + il // 2 for il, q, m in order],
            )
            for rh in range(2)
        ]
    )
    place = np.zeros((OCC, NP * OCC, 2 * NP * HALF), np.float32)
    for il in range(OCC):
        for q in range(NP):
            for jl in range(OCC):
                rh = (il + jl) % 2
                place[il, q * OCC + jl, rh * NP * HALF + q * HALF + jl // 2] = 1.0
    blocks = one_hot(NP, [q for _, q, _ in order])
    return send, own, mirror, place, blocks


SEND, OWN, MIRROR, PLACE, BLOCKS = tables()


def dot(a, b):
    return jnp.dot(a, b, preferred_element_type=jnp.float32)


def body(amplitudes, integrals, amp_pattern, int_pattern):
    rows, kcd = amplitudes.shape
    cols = integrals.shape[1]
    bf = jnp.bfloat16
    p = lax.axis_index(PAIR)
    v = lax.axis_index(VIRT)
    y = lax.axis_index("y")
    z = lax.axis_index("z")
    width = kcd // NZ

    n = jnp.arange(2 * PAD)
    rh, n = n // PAD, n % PAD
    k, m = n // HALF, n % HALF
    il = (OCC * v + k) // NP
    source = jnp.where(n < PER, k * OCC + 2 * m + (il + rh) % 2, -1)
    pick = (source[:, None] == jnp.arange(rows)[None, :]).astype(bf)
    split = dot(pick, amplitudes).astype(bf)
    first = (
        split.reshape(2, PAD, NZ, 2, LANES).transpose(0, 3, 2, 1, 4).reshape(NP, PAD, LANES)
    )
    held = lax.all_to_all(first, VIRT, split_axis=0, concat_axis=0, tiled=True)
    held = held.reshape(NP * PAD, LANES)

    second = dot(jnp.asarray(SEND, bf), held).astype(bf).reshape(NP, PAD, LANES)
    other = lax.all_to_all(second, PAIR, split_axis=0, concat_axis=0, tiled=True)
    other = other.reshape(NP * PAD, LANES)

    pattern = lax.dynamic_index_in_dim(
        amp_pattern, z * width // TP, 2, keepdims=False
    ).astype(jnp.float32)
    mine = lax.dynamic_index_in_dim(pattern, p, 0, keepdims=False)
    theirs = lax.dynamic_index_in_dim(pattern, p, 1, keepdims=False)
    masks = dot(jnp.asarray(BLOCKS, bf), jnp.stack([mine, theirs], 1).astype(bf))
    mirror = lax.dynamic_index_in_dim(jnp.asarray(MIRROR, bf), y // 2, 0, keepdims=False)
    diff = dot(jnp.asarray(OWN, bf), held) * masks[:, :1] - dot(mirror, other) * masks[:, 1:]
    diff = diff.astype(bf)

    gathered = lax.all_gather(diff, "y", axis=0, tiled=False)
    pieces = [jnp.concatenate([gathered[2 * r], gathered[2 * r + 1]], 1) for r in range(2)]

    col_mask = lax.dynamic_index_in_dim(int_pattern, v * cols // TP, 1, keepdims=False)
    weighted = integrals * jnp.repeat(col_mask, TP).astype(bf)[:, None]

    sign = 1 - 2 * lax.axis_index("core")

    def term(c, distance):
        start = lax.rem(z + sign * distance + NZ, NZ) * width
        return dot(c, lax.dynamic_slice_in_dim(weighted, start, width, 0))

    def shift(step):
        return [
            (c * NZ + i, c * NZ + (i + (1 - 2 * c) * step) % NZ)
            for c in range(2)
            for i in range(NZ)
        ]

    ways = (shift(1), shift(-1))
    front = [list(pieces), list(pieces)]
    totals = [term(c, 0) for c in pieces]
    for step in range(1, NZ // 2 + 1):
        arrived = front[0][0]
        for i in range(2):
            for w in range(2):
                if step == NZ // 2 and w != i:
                    continue
                if step == NZ // 2 and i == 1:
                    front[1][1], _ = lax.optimization_barrier((front[1][1], arrived))
                front[w][i] = lax.ppermute(front[w][i], ("core", "z"), ways[w])
                totals[i] = totals[i] + term(front[w][i], -step if w == 0 else step)
    both = jnp.concatenate([t.astype(bf).reshape(OCC, NP * HALF, cols) for t in totals], 1)
    out = jnp.einsum(
        "bij,bjk->bik", jnp.asarray(PLACE, bf), both, preferred_element_type=jnp.float32
    )
    return out.astype(bf).reshape(OCC * NP * OCC, cols)


def solution(mesh):
    fine = Mesh(mesh.devices.reshape(8, 2, 2, NY, NZ), AXES)
    placed = (P(AXES, None), P(None, VIRT), P(), P())
    return jax.shard_map(
        body, mesh=fine, in_specs=placed, out_specs=P(PAIR, VIRT), check_vma=False
    )
```
